1024 devices in a mesh: fsdp: 16 (over y, core), grp: 64 (over x, z).
Axes of the slice: x: 4, y: 8, z: 16, core: 2. Of those that a mesh axis runs over, the one named last changes fastest.
Arguments:
- grad: bfloat16 [64, 512, 8192], P('grp', 'fsdp'), may hold values from -30 to 30
- table: int32 [64, 16], P('grp'), may hold values from 0 to 15, each once within a row
- left_stat: bfloat16 [64, 16, 512, 512], P('grp', 'fsdp'), may hold values from -4 to 4, as said below
- right_stat: bfloat16 [64, 16, 512, 512], P('grp', 'fsdp'), may hold values from -4 to 4, as said below
- left_basis: bfloat16 [64, 16, 512, 512], P('grp', 'fsdp'), may hold values from -4 to 4, as said below
- right_basis: bfloat16 [64, 16, 512, 512], P('grp', 'fsdp'), may hold values from -4 to 4, as said below
- row_moment: float32 [64, 16, 512], P('grp', 'fsdp'), may hold values from 0.05 to 1
- col_moment: float32 [64, 16, 512], P('grp', 'fsdp'), may hold values from 0.05 to 1
Outputs:
- update: bfloat16 [64, 512, 8192], P('grp', 'fsdp')
- row_next: float32 [64, 16, 512], P('grp', 'fsdp')
- col_next: float32 [64, 16, 512], P('grp', 'fsdp')
The draws below stay inside these ranges and needn't reach their ends.
Inputs may be any that keep to these rules, and one draw needn't show every extreme that they name: Each row of table lists every owner 0 to 15 once. `left_stat`: symmetric with a dominant diagonal. `right_stat`: symmetric with a dominant diagonal. `left_basis`: nonsingular. `right_basis`: nonsingular.
All inputs are finite; a program needn't handle non-finite values.
Results may differ from the reference program's by a relative error of at most 0.01.
Values may be sent and summed in bfloat16 or wider, within the bound.
No kernel may reach another device: no remote copies, remote signals or barrier semaphores. Data moves between devices by JAX's collectives and lax.ppermute only.
A program may use at most 32 MiB of HBM per device.

```python
import math
import jax
import jax.numpy as jnp
from jax import lax

B = 512
NF = 16
GROUPS = 64


def symmetric_draw(key):
    noise = jax.random.normal(key, (GROUPS, NF, B, B), jnp.float32)
    sym = (noise + jnp.swapaxes(noise, 2, 3)) / jnp.sqrt(2.0)
    spread = 0.5
    result = 2.0 * jnp.eye(B, dtype=jnp.float32) + spread / jnp.sqrt(1.0 * B) * sym
    return jnp.clip(result, -4.0, 4.0).astype(jnp.bfloat16)


def basis_draw(key):
    noise = jax.random.normal(key, (GROUPS, NF, B, B), jnp.float32)
    spread = 0.5
    result = jnp.eye(B, dtype=jnp.float32) + spread / jnp.sqrt(1.0 * B) * noise
    return jnp.clip(result, -4.0, 4.0).astype(jnp.bfloat16)


def draw_grad(key, part):
    inner_key = jax.random.fold_in(key, 21)
    base = jnp.clip(jax.random.normal(inner_key, (GROUPS, B, NF * B), jnp.float32), -6.0, 6.0)
    lowest = 0.4
    highest = 2.0
    group_scale = jnp.exp(jnp.linspace(jnp.log(lowest), jnp.log(highest), GROUPS, dtype=jnp.float32))
    row_scale = jnp.exp(jnp.linspace(jnp.log(0.6), jnp.log(1.5), B, dtype=jnp.float32))
    result = base * group_scale[:, None, None] * row_scale[None, :, None]
    return result.astype(jnp.bfloat16)


def draw_left_stat(key, part):
    return symmetric_draw(jax.random.fold_in(key, 11))


def draw_right_stat(key, part):
    return symmetric_draw(jax.random.fold_in(key, 12))


def draw_left_basis(key, part):
    return basis_draw(jax.random.fold_in(key, 13))


def draw_right_basis(key, part):
    return basis_draw(jax.random.fold_in(key, 14))


def shard_levels(stream_key, dims, split, smallest, high):
    level = 1.0
    for position, blocks in split:
        heights = jax.random.uniform(jax.random.fold_in(jax.random.fold_in(stream_key, 6), position), (blocks,), jnp.float32, smallest / len(split), high / len(split))
        level = level * jnp.repeat(jnp.exp(heights), dims[position] // blocks).reshape((-1,) + (1,) * (len(dims) - 1 - position))
    return level


def setup_inputs(seed: int = 0) -> dict:
    splits = jax.random.split(jax.random.key(seed), 9)
    grad = draw_grad(jax.random.fold_in(splits[8], 71), 0)
    table = jax.vmap(lambda own: jax.random.permutation(own, NF))(jax.random.split(splits[1], GROUPS)).reshape((GROUPS, NF)).astype(jnp.int32)
    left_stat = draw_left_stat(jax.random.fold_in(splits[8], 71), 0)
    right_stat = draw_right_stat(jax.random.fold_in(splits[8], 71), 0)
    left_basis = draw_left_basis(jax.random.fold_in(splits[8], 71), 0)
    right_basis = draw_right_basis(jax.random.fold_in(splits[8], 71), 0)
    row_moment = jnp.clip(jnp.exp(math.log(1.0) - 2.9957323 * jax.random.uniform(splits[6], (GROUPS, NF, B), jnp.float32) ** shard_levels(splits[6], (GROUPS, NF, B), ((0, 64), (1, 16)), -0.2, 0.2)), 0.05, 1.0)
    col_moment = jnp.clip(jnp.exp(math.log(1.0) - 2.9957323 * jax.random.uniform(splits[7], (GROUPS, NF, B), jnp.float32) ** shard_levels(splits[7], (GROUPS, NF, B), ((0, 64), (1, 16)), -0.2, 0.2)), 0.05, 1.0)
    return {"grad": grad, "table": table, "left_stat": left_stat, "right_stat": right_stat, "left_basis": left_basis, "right_basis": right_basis, "row_moment": row_moment, "col_moment": col_moment}


DECAY_STAT = 0.95
DECAY_MOMENT = 0.95
CLIP_RMS = 0.5
EPSILON = 1e-08

def refresh(stat, gram, basis, clip):
    new_stat = DECAY_STAT * stat.astype(jnp.float32) + (1.0 - DECAY_STAT) * clip * clip * gram
    product = jnp.dot(new_stat, basis.astype(jnp.float32), precision=lax.Precision.HIGHEST)
    inner = jnp.dot(product.T, product, precision=lax.Precision.HIGHEST)
    factor = jnp.linalg.cholesky(inner)
    ortho = jax.scipy.linalg.solve_triangular(factor, product.T, lower=True).T
    return ortho.astype(jnp.bfloat16)

def soap_block(block, clip, left_stat, right_stat, left_basis, right_basis, row_moment, col_moment):
    left_gram = jnp.dot(block.astype(jnp.float32), block.T.astype(jnp.float32), preferred_element_type=jnp.float32)
    right_gram = jnp.dot(block.T.astype(jnp.float32), block.astype(jnp.float32), preferred_element_type=jnp.float32)
    left_new = refresh(left_stat, left_gram, left_basis, clip)
    right_new = refresh(right_stat, right_gram, right_basis, clip)
    half = jnp.dot(left_new.T.astype(jnp.float32), block.astype(jnp.float32), preferred_element_type=jnp.float32).astype(jnp.bfloat16)
    rotated = clip * jnp.dot(half.astype(jnp.float32), right_new.astype(jnp.float32), preferred_element_type=jnp.float32)
    square = rotated * rotated
    row_next = DECAY_MOMENT * row_moment + (1.0 - DECAY_MOMENT) * lax.optimization_barrier(jnp.mean(square, axis=1))
    col_next = DECAY_MOMENT * col_moment + (1.0 - DECAY_MOMENT) * lax.optimization_barrier(jnp.mean(square, axis=0))
    second = row_next[:, None] * col_next[None, :] / jnp.mean(row_next)
    normed = (rotated / (jnp.sqrt(second) + EPSILON)).astype(jnp.bfloat16)
    back = jnp.dot(left_new.astype(jnp.float32), normed.astype(jnp.float32), preferred_element_type=jnp.float32).astype(jnp.bfloat16)
    update = jnp.dot(back.astype(jnp.float32), right_new.T.astype(jnp.float32), preferred_element_type=jnp.float32).astype(jnp.bfloat16)
    return (update, row_next, col_next)

def reference(grad, table, left_stat, right_stat, left_basis, right_basis, row_moment, col_moment):
    total = jnp.sum(jnp.square(grad.astype(jnp.float32)))
    count = GROUPS * NF * B * B
    clip = CLIP_RMS / jnp.sqrt(total / count + 1e-06)
    inverse = jnp.argsort(table, axis=1).astype(jnp.int32).reshape(GROUPS * NF)
    groups_of = (jnp.arange(GROUPS * NF, dtype=jnp.int32) // NF).astype(jnp.int32)

    def one_owner(items):
        group, column, lstat, rstat, lbasis, rbasis, rmom, cmom = items
        start = (column * B).astype(jnp.int32)
        block = lax.dynamic_slice(grad, (group, jnp.int32(0), start), (1, B, B))[0]
        return soap_block(block, clip, lstat, rstat, lbasis, rbasis, rmom, cmom)
    blocks, row_next, col_next = lax.map(one_owner, (groups_of, inverse, left_stat.reshape(GROUPS * NF, B, B), right_stat.reshape(GROUPS * NF, B, B), left_basis.reshape(GROUPS * NF, B, B), right_basis.reshape(GROUPS * NF, B, B), row_moment.reshape(GROUPS * NF, B), col_moment.reshape(GROUPS * NF, B)))
    blocks = blocks.reshape(GROUPS, NF, B, B)
    by_column = jnp.take_along_axis(blocks, table[:, :, None, None].astype(jnp.int32), axis=1)
    update = by_column.transpose(0, 2, 1, 3).reshape(GROUPS, B, NF * B)
    return (update, row_next.reshape(GROUPS, NF, B), col_next.reshape(GROUPS, NF, B))
```

```python
import jax
import jax.numpy as jnp
from jax import lax
from jax.experimental import pallas as pl
from jax.experimental.pallas import tpu as pltpu
from jax.sharding import PartitionSpec as P

DECAY_STAT = 0.95
DECAY_MOMENT = 0.95
CLIP_RMS = 0.5
EPSILON = 1e-08
F32 = jnp.float32
BF16 = jnp.bfloat16
TILE = 8
NB = 128
NT = NB // TILE
NN = (((1,), (0,)), ((), ()))
NT_DIMS = (((1,), (1,)), ((), ()))
TN = (((0,), (0,)), ((), ()))


def mm(a, b, dims=NN):
    return lax.dot_general(a, b, dims, preferred_element_type=F32)


def mm_full(a, b, dims=NN):
    return lax.dot_general(a, b, dims, precision=lax.Precision.HIGHEST, preferred_element_type=F32)


def split3(x):
    high = x.astype(BF16)
    rest = x - high.astype(F32)
    mid = rest.astype(BF16)
    low = (rest - mid.astype(F32)).astype(BF16)
    return high, mid, low


def mm_split(x, exact, dims=NN):
    high, mid, low = split3(x)
    return mm(high, exact, dims) + mm(mid, exact, dims) + mm(low, exact, dims)


def lane(x, c):
    return jnp.broadcast_to(x[:, c : c + 1], (TILE, NB))


def row(x, r):
    return jnp.broadcast_to(x[r : r + 1, :], (TILE, NB))


def factor_steps(get, aug, side, out):
    lanes = lax.broadcasted_iota(jnp.int32, (TILE, NB), 1)
    subs = lax.broadcasted_iota(jnp.int32, (TILE, NB), 0)

    def at(i):
        return (side, slice(TILE * i, TILE * i + TILE), slice(None))

    for i in range(NT):
        aug[at(i)] = jnp.where(lanes == subs + TILE * i, 1.0, 0.0).astype(F32)
    for k in range(NT):
        base = TILE * k
        tile = get[at(k)]
        both = aug[at(k)]
        forward = both
        cols = [lane(tile, base + j) for j in range(TILE)]
        pivots = jnp.ones((TILE, NB), F32)
        for j in range(TILE):
            pivot = row(cols[j], j)
            pivots = jnp.where(subs == j, pivot, pivots)
            mult = cols[j] * (1.0 / pivot)
            around = jnp.where(subs == j, 0.0, mult)
            below = jnp.where(subs > j, mult, 0.0)
            for q in range(j + 1, TILE):
                cols[q] = cols[q] - around * row(cols[q], j)
            both_row = row(both, j)
            tile = tile - around * row(tile, j)
            both = both - around * both_row
            forward = forward - below * both_row
            yield
        inverse = 1.0 / pivots
        out[at(k)] = forward * lax.rsqrt(pivots)
        tile = tile * inverse
        both = both * inverse
        tile_rows = [row(tile, j) for j in range(TILE)]
        both_rows = [row(both, j) for j in range(TILE)]
        for i in range(k + 1, NT):
            old = get[at(i)]
            left = [lane(old, base + j) for j in range(TILE)]
            first = [left[j] * tile_rows[j] for j in range(TILE)]
            second = [left[j] * both_rows[j] for j in range(TILE)]
            while len(first) > 1:
                first = [first[q] + first[q + 1] for q in range(0, len(first), 2)]
                second = [second[q] + second[q + 1] for q in range(0, len(second), 2)]
            get[at(i)] = old - first[0]
            aug[at(i)] = aug[at(i)] - second[0]
        yield


def interleave(steps):
    steps = list(steps)
    while steps:
        steps = [s for s in steps if next(s, steps) is not steps]


def prep_kernel(table_ref, grad_ref, out_ref, sum_ref):
    owners, my_rows, order = out_ref.shape
    total = jnp.zeros((my_rows, order), F32)
    for j in range(owners):
        part = grad_ref[:, j * order : (j + 1) * order]
        out_ref[table_ref[0, j]] = part
        wide = part.astype(F32)
        total = total + wide * wide
    sum_ref[...] = jnp.sum(total).reshape(1, 1)


def place_kernel(table_ref, back_ref, out_ref):
    owners, my_rows, order = back_ref.shape
    for j in range(owners):
        out_ref[:, j * order : (j + 1) * order] = back_ref[table_ref[0, j]]


def early_kernel(left_stat, right_stat, left_basis, right_basis, basis_t, stat_part):
    for side, (stat, basis) in enumerate(((left_stat, left_basis), (right_stat, right_basis))):
        turned = basis[...].T
        basis_t[side] = turned
        stat_part[side] = DECAY_STAT * mm(turned, stat[...])


def gram_kernel(block_ref, basis_t, gram_part):
    block = block_ref[...]
    gram_part[0] = (1.0 - DECAY_STAT) * mm_split(mm(basis_t[0], block), block, NT_DIMS)
    gram_part[1] = (1.0 - DECAY_STAT) * mm_split(mm(basis_t[1], block, NT_DIMS), block)


def main_kernel(
    clip_ref, block_ref, stat_part, gram_part, row_ref, col_ref, update_ref, row_out, col_out,
    s_ref, a_ref, t_ref, aug_ref, w_ref, q_ref,
):
    order = block_ref.shape[0]
    clip = clip_ref[0, 0]
    for side in range(2):
        a = stat_part[side] + (clip * clip) * gram_part[side]
        a_ref[side] = a
        high, mid, low = split3(a)
        for k in range(order // NB):
            part = slice(k * NB, order)
            mine = slice(k * NB, (k + 1) * NB)
            total = mm(low[mine], high[part], NT_DIMS) + mm(high[mine], low[part], NT_DIMS)
            total = total + mm(mid[mine], mid[part], NT_DIMS)
            total = total + mm(mid[mine], high[part], NT_DIMS) + mm(high[mine], mid[part], NT_DIMS)
            s_ref[side, mine, part] = total + mm(high[mine], high[part], NT_DIMS)

    for k in range(order // NB):
        mine = slice(k * NB, (k + 1) * NB)
        for side in range(2):
            t_ref[side] = s_ref[side, mine, mine]
        interleave([factor_steps(t_ref, aug_ref, side, w_ref) for side in range(2)])
        for side in range(2):
            turned = mm_full(w_ref[side], a_ref[side, mine, :])
            q_ref[side, mine, :] = turned.astype(BF16)
            if (k + 1) * NB < order:
                rest = slice((k + 1) * NB, order)
                panel = mm_full(w_ref[side], s_ref[side, mine, rest])
                panel_t = panel.T
                s_ref[side, rest, rest] = s_ref[side, rest, rest] - mm_full(panel_t, panel)
                a_ref[side, rest, :] = a_ref[side, rest, :] - mm_full(panel_t, turned)

    block = block_ref[...]
    left_t = q_ref[0]
    right_t = q_ref[1]
    half = mm(left_t, block).astype(BF16)
    rotated = clip * mm(half, right_t, NT_DIMS)
    square = rotated * rotated
    col_next = DECAY_MOMENT * col_ref[...] + (1.0 - DECAY_MOMENT) * jnp.mean(square, axis=0, keepdims=True)
    old_rows = jnp.broadcast_to(row_ref[...], (NB, order)).T
    row_mean = jnp.broadcast_to(jnp.mean(square, axis=1, keepdims=True), (order, NB))
    row_next = DECAY_MOMENT * old_rows + (1.0 - DECAY_MOMENT) * row_mean
    col_out[...] = col_next
    across = row_next.T[0:1, :]
    row_out[...] = across
    second = row_next[:, 0:1] * col_next / jnp.mean(across)
    normed = (rotated / (jnp.sqrt(second) + EPSILON)).astype(BF16)
    back = mm(left_t, normed, TN).astype(BF16)
    update_ref[...] = mm(back, right_t).astype(BF16)


VMEM = pl.BlockSpec(memory_space=pltpu.VMEM)
SMEM = pl.BlockSpec(memory_space=pltpu.SMEM)


def call(kernel, out_shapes, in_specs, out_specs, scratch=(), flops=0, moved=0):
    return pl.pallas_call(
        kernel,
        out_shape=out_shapes,
        in_specs=in_specs,
        out_specs=out_specs,
        scratch_shapes=list(scratch),
        compiler_params=pltpu.CompilerParams(vmem_limit_bytes=48 * 2**20),
        cost_estimate=pl.CostEstimate(flops=flops, bytes_accessed=moved, transcendentals=0),
    )


def shards(grad, table, left_stat, right_stat, left_basis, right_basis, row_moment, col_moment):
    order = left_stat.shape[-1]
    owners = lax.axis_size("fsdp")
    groups = lax.axis_size("grp")
    my_rows = grad.shape[1]
    shape = jax.ShapeDtypeStruct
    cube = 2 * order**3

    outgoing, local = call(
        prep_kernel,
        (shape((owners, my_rows, order), BF16), shape((1, 1), F32)),
        [SMEM, VMEM],
        (VMEM, VMEM),
        moved=4 * owners * my_rows * order,
    )(table, grad[0])
    block = lax.all_to_all(outgoing, "fsdp", split_axis=0, concat_axis=0, tiled=True).reshape(order, order)

    basis_t, stat_part = call(
        early_kernel,
        (shape((2, order, order), BF16), shape((2, order, order), F32)),
        [VMEM] * 4,
        (VMEM, VMEM),
        flops=2 * cube,
        moved=16 * order * order,
    )(left_stat[0, 0], right_stat[0, 0], left_basis[0, 0], right_basis[0, 0])

    def sum_over(value, axis, size):
        sent = jnp.broadcast_to(value.reshape(1, 1, 1), (size, 1, 1))
        return jnp.sum(lax.all_to_all(sent, axis, 0, 0, tiled=True))

    total = sum_over(sum_over(local, "fsdp", owners), "grp", groups)
    count = float(groups * owners * order * order)
    clip = CLIP_RMS / jnp.sqrt(total / count + 1e-06)

    gram_part = call(
        gram_kernel,
        shape((2, order, order), F32),
        [VMEM, VMEM],
        VMEM,
        flops=8 * cube,
        moved=14 * order * order,
    )(block, basis_t)

    wide = pltpu.VMEM((2, order, order), F32)
    small = pltpu.VMEM((2, NB, NB), F32)
    update, row_next, col_next = call(
        main_kernel,
        (shape((order, order), BF16), shape((1, order), F32), shape((1, order), F32)),
        [SMEM] + [VMEM] * 5,
        (VMEM, VMEM, VMEM),
        [wide, wide, small, small, small, pltpu.VMEM((2, order, order), BF16)],
        flops=40 * cube,
        moved=20 * order * order,
    )(clip.reshape(1, 1), block, stat_part, gram_part, row_moment[0], col_moment[0])

    pieces = update.reshape(owners, my_rows, order)
    returned = lax.all_to_all(pieces, "fsdp", split_axis=0, concat_axis=0, tiled=True)
    placed = call(
        place_kernel,
        shape((my_rows, owners * order), BF16),
        [SMEM, VMEM],
        VMEM,
        moved=4 * owners * my_rows * order,
    )(table, returned)
    return (placed[None], row_next[None], col_next[None])


def solution(mesh):
    in_specs = (
        P("grp", "fsdp", None),
        P("grp", None),
        P("grp", "fsdp", None, None),
        P("grp", "fsdp", None, None),
        P("grp", "fsdp", None, None),
        P("grp", "fsdp", None, None),
        P("grp", "fsdp", None),
        P("grp", "fsdp", None),
    )
    out_specs = (P("grp", "fsdp", None), P("grp", "fsdp", None), P("grp", "fsdp", None))
    return jax.shard_map(shards, mesh=mesh, in_specs=in_specs, out_specs=out_specs, check_vma=False)
```

```python
import functools

import jax
import jax.numpy as jnp
from jax import lax
from jax.experimental import pallas as pl
from jax.experimental.pallas import tpu as pltpu
from jax.sharding import PartitionSpec as P

DECAY_STAT = 0.95
DECAY_MOMENT = 0.95
CLIP_RMS = 0.5
EPSILON = 1e-08
F32 = jnp.float32
BF16 = jnp.bfloat16
TILE = 8
NB = 128
NT = NB // TILE
EXTRA = 16
NN = (((1,), (0,)), ((), ()))
NT_DIMS = (((1,), (1,)), ((), ()))
TN = (((0,), (0,)), ((), ()))


def mm(a, b, dims=NN):
    return lax.dot_general(a, b, dims, preferred_element_type=F32)


def mm_full(a, b, dims=NN):
    return lax.dot_general(a, b, dims, precision=lax.Precision.HIGHEST, preferred_element_type=F32)


def split3(x):
    high = x.astype(BF16)
    rest = x - high.astype(F32)
    mid = rest.astype(BF16)
    low = (rest - mid.astype(F32)).astype(BF16)
    return high, mid, low


def mm_split(x, exact, dims=NN):
    high, mid, low = split3(x)
    return mm(high, exact, dims) + mm(mid, exact, dims) + mm(low, exact, dims)


def lane(x, c):
    return jnp.broadcast_to(x[:, c : c + 1], (TILE, NB))


def row(x, r):
    return jnp.broadcast_to(x[r : r + 1, :], (TILE, NB))


def factor_steps(get, aug, side, out, slot):
    lanes = lax.broadcasted_iota(jnp.int32, (TILE, NB), 1)
    subs = lax.broadcasted_iota(jnp.int32, (TILE, NB), 0)

    def at(i):
        return (side, slice(TILE * i, TILE * i + TILE), slice(None))

    for i in range(NT):
        aug[at(i)] = jnp.where(lanes == subs + TILE * i, 1.0, 0.0).astype(F32)
    for k in range(NT):
        base = TILE * k
        tile = get[at(k)]
        both = aug[at(k)]
        forward = both
        cols = [lane(tile, base + j) for j in range(TILE)]
        pivots = jnp.ones((TILE, NB), F32)
        for j in range(TILE):
            pivot = row(cols[j], j)
            pivots = jnp.where(subs == j, pivot, pivots)
            mult = cols[j] * (1.0 / pivot)
            around = jnp.where(subs == j, 0.0, mult)
            below = jnp.where(subs > j, mult, 0.0)
            for q in range(j + 1, TILE):
                cols[q] = cols[q] - around * row(cols[q], j)
            both_row = row(both, j)
            tile = tile - around * row(tile, j)
            both = both - around * both_row
            forward = forward - below * both_row
            yield
        inverse = 1.0 / pivots
        out[slot + side, TILE * k : TILE * k + TILE, :] = forward * lax.rsqrt(pivots)
        tile = tile * inverse
        both = both * inverse
        tile_rows = [row(tile, j) for j in range(TILE)]
        both_rows = [row(both, j) for j in range(TILE)]
        for i in range(k + 1, NT):
            old = get[at(i)]
            left = [lane(old, base + j) for j in range(TILE)]
            first = [left[j] * tile_rows[j] for j in range(TILE)]
            second = [left[j] * both_rows[j] for j in range(TILE)]
            while len(first) > 1:
                first = [first[q] + first[q + 1] for q in range(0, len(first), 2)]
                second = [second[q] + second[q + 1] for q in range(0, len(second), 2)]
            get[at(i)] = old - first[0]
            aug[at(i)] = aug[at(i)] - second[0]
        yield


def interleave(steps, later, every):
    steps, later, count = list(steps), list(later), 0
    while steps or later:
        steps = [s for s in steps if next(s, steps) is not steps]
        count += 1
        if count % every == 0 or not steps:
            later = [s for s in later if next(s, later) is not later]


def prep_kernel(table_ref, grad_ref, out_ref):
    owners, _, width = out_ref.shape
    my_rows = grad_ref.shape[0]
    order = grad_ref.shape[1] // owners
    total = jnp.zeros((my_rows, order), F32)
    for j in range(owners):
        part = grad_ref[:, j * order : (j + 1) * order]
        for c in range(order // width):
            out_ref[table_ref[0, j], c * my_rows : (c + 1) * my_rows, :] = part[:, c * width : (c + 1) * width]
        wide = part.astype(F32)
        total = total + wide * wide
    high, mid, low = split3(jnp.broadcast_to(jnp.sum(total).reshape(1, 1), (EXTRA, width)))
    rows = lax.broadcasted_iota(jnp.int32, (EXTRA, width), 0)
    extra = jnp.where(rows == 0, high.astype(F32), jnp.where(rows == 1, mid.astype(F32), low.astype(F32)))
    extra = jnp.where(rows < 3, extra, 0.0).astype(BF16)
    for o in range(owners):
        out_ref[o, order // width * my_rows :, :] = extra


def sum_kernel(block_ref, sum_ref):
    owners, height, width = block_ref.shape
    total = jnp.zeros((EXTRA, width), F32)
    for o in range(owners):
        total = total + block_ref[o, height - EXTRA :, :].astype(F32)
    sum_ref[...] = jnp.broadcast_to(jnp.sum(total, axis=0).reshape(1, 1, width), sum_ref.shape)


def place_kernel(table_ref, back_ref, out_ref):
    owners, my_rows, order = back_ref.shape
    for j in range(owners):
        out_ref[:, j * order : (j + 1) * order] = back_ref[table_ref[0, j]]


def early_kernel(left_stat, right_stat, left_basis, right_basis, basis_t, stat_part):
    for side, (stat, basis) in enumerate(((left_stat, left_basis), (right_stat, right_basis))):
        turned = basis[...].T
        basis_t[side] = turned
        stat_part[side] = DECAY_STAT * mm(turned, stat[...])


def gram_kernel(recv_ref, basis_t, block_ref, gram_part):
    owners, height, width = recv_ref.shape
    order = block_ref.shape[0]
    my_rows = order // owners
    for o in range(owners):
        for c in range(order // width):
            piece = recv_ref[o, c * my_rows : (c + 1) * my_rows, :]
            block_ref[o * my_rows : (o + 1) * my_rows, c * width : (c + 1) * width] = piece
    block = block_ref[...]
    gram_part[0] = (1.0 - DECAY_STAT) * mm_split(mm(basis_t[0], block), block, NT_DIMS)
    gram_part[1] = (1.0 - DECAY_STAT) * mm_split(mm(basis_t[1], block, NT_DIMS), block)


def main_kernel(
    count, sum_ref, block_ref, stat_part, gram_part, row_ref, col_ref, update_ref, row_out, col_out,
    s_ref, a_ref, t_ref, aug_ref, w_ref, p_ref, q_ref,
):
    order = block_ref.shape[0]
    blocks = order // NB
    total = jnp.sum(jnp.sum(sum_ref[...], axis=0), axis=1, keepdims=True) * (1.0 / sum_ref.shape[2])
    clip = CLIP_RMS / jnp.sqrt(total / count + 1e-06)
    for side in range(2):
        a = stat_part[side] + (clip * clip) * gram_part[side]
        a_ref[side] = a
        high, mid, low = split3(a)
        for k in range(blocks):
            part = slice(k * NB, order)
            mine = slice(k * NB, (k + 1) * NB)
            near = mm(low[mine], high[part], NT_DIMS) + mm(high[mine], low[part], NT_DIMS)
            near = near + mm(mid[mine], mid[part], NT_DIMS)
            near = near + mm(mid[mine], high[part], NT_DIMS) + mm(high[mine], mid[part], NT_DIMS)
            s_ref[side, mine, part] = near + mm(high[mine], high[part], NT_DIMS)

    def at(k):
        return slice(k * NB, (k + 1) * NB)

    def finish(k, side):
        w = w_ref[k % 2 * 2 + side]
        rest = slice((k + 1) * NB, order)
        if k + 2 < blocks:
            far = slice((k + 2) * NB, order)
            p_ref[side, :, far] = mm_full(w, s_ref[side, at(k), far])
            yield
        if k + 1 < blocks:
            panel_t = p_ref[side, :, rest].T
        half = order // 2
        for c in range(2):
            cols = slice(c * half, (c + 1) * half)
            turned = mm_full(w, a_ref[side, at(k), cols])
            q_ref[side, at(k), cols] = turned.astype(BF16)
            yield
            if k + 1 < blocks:
                a_ref[side, rest, cols] = a_ref[side, rest, cols] - mm_full(panel_t, turned)
                yield
        for i in range(k + 1, blocks):
            first = max(i, k + 2)
            if first < blocks:
                cols = slice(first * NB, order)
                panel_i = panel_t[(i - k - 1) * NB : (i - k) * NB]
                s_ref[side, at(i), cols] = s_ref[side, at(i), cols] - mm_full(panel_i, p_ref[side, :, cols])
                yield

    waiting = []
    for k in range(blocks):
        slot = k % 2 * 2
        for side in range(2):
            if k == 0:
                t_ref[side] = s_ref[side, at(0), at(0)]
        interleave([factor_steps(t_ref, aug_ref, side, w_ref, slot) for side in range(2)], waiting, 8)
        if k + 1 < blocks:
            for side in range(2):
                panel = mm_full(w_ref[slot + side], s_ref[side, at(k), at(k + 1)])
                p_ref[side, :, at(k + 1)] = panel
                t_ref[side] = s_ref[side, at(k + 1), at(k + 1)] - mm_full(panel.T, panel)
        waiting = [finish(k, side) for side in range(2)]
    interleave([], waiting, 1)

    block = block_ref[...]
    left_t = q_ref[0]
    right_t = q_ref[1]
    half = mm(left_t, block).astype(BF16)
    rotated = clip * mm(half, right_t, NT_DIMS)
    square = rotated * rotated
    col_next = DECAY_MOMENT * col_ref[...] + (1.0 - DECAY_MOMENT) * jnp.mean(square, axis=0, keepdims=True)
    old_rows = jnp.broadcast_to(row_ref[...], (NB, order)).T
    row_mean = jnp.broadcast_to(jnp.mean(square, axis=1, keepdims=True), (order, NB))
    row_next = DECAY_MOMENT * old_rows + (1.0 - DECAY_MOMENT) * row_mean
    col_out[...] = col_next
    across = row_next.T[0:1, :]
    row_out[...] = across
    second = row_next[:, 0:1] * col_next / jnp.mean(across)
    normed = (rotated / (jnp.sqrt(second) + EPSILON)).astype(BF16)
    back = mm(left_t, normed, TN).astype(BF16)
    update_ref[...] = mm(back, right_t).astype(BF16)


VMEM = pl.BlockSpec(memory_space=pltpu.VMEM)
SMEM = pl.BlockSpec(memory_space=pltpu.SMEM)


def call(kernel, out_shapes, in_specs, out_specs, scratch=(), flops=0, moved=0, limit=12):
    return pl.pallas_call(
        kernel,
        out_shape=out_shapes,
        in_specs=in_specs,
        out_specs=out_specs,
        scratch_shapes=list(scratch),
        compiler_params=pltpu.CompilerParams(vmem_limit_bytes=limit * 2**20),
        cost_estimate=pl.CostEstimate(flops=flops, bytes_accessed=moved, transcendentals=0),
    )


def shards(grad, table, left_stat, right_stat, left_basis, right_basis, row_moment, col_moment):
    order = left_stat.shape[-1]
    owners = lax.axis_size("fsdp")
    groups = lax.axis_size("grp")
    my_rows = grad.shape[1]
    shape = jax.ShapeDtypeStruct
    cube = 2 * order**3

    outgoing = call(
        prep_kernel,
        shape((owners, order // NB * my_rows + EXTRA, NB), BF16),
        [SMEM, VMEM],
        VMEM,
        moved=4 * owners * my_rows * order,
    )(table, grad[0])
    received = lax.all_to_all(outgoing, "fsdp", split_axis=0, concat_axis=0, tiled=True)

    basis_t, stat_part = call(
        early_kernel,
        (shape((2, order, order), BF16), shape((2, order, order), F32)),
        [VMEM] * 4,
        (VMEM, VMEM),
        flops=2 * cube,
        moved=16 * order * order,
    )(left_stat[0, 0], right_stat[0, 0], left_basis[0, 0], right_basis[0, 0])

    mine = call(sum_kernel, shape((groups, 1, NB), F32), [VMEM], VMEM, moved=64 * owners * NB)(received)
    sums = lax.all_to_all(mine, "grp", split_axis=0, concat_axis=0, tiled=True)

    block, gram_part = call(
        gram_kernel,
        (shape((order, order), BF16), shape((2, order, order), F32)),
        [VMEM, VMEM],
        (VMEM, VMEM),
        flops=8 * cube,
        moved=14 * order * order,
    )(received, basis_t)

    wide = pltpu.VMEM((2, order, order), F32)
    small = pltpu.VMEM((2, NB, NB), F32)
    update, row_next, col_next = call(
        functools.partial(main_kernel, float(groups * owners * order * order)),
        (shape((order, order), BF16), shape((1, order), F32), shape((1, order), F32)),
        [VMEM] * 6,
        (VMEM, VMEM, VMEM),
        [wide, wide, small, small, pltpu.VMEM((4, NB, NB), F32), pltpu.VMEM((2, NB, order), F32), pltpu.VMEM((2, order, order), BF16)],
        flops=40 * cube,
        moved=20 * order * order,
        limit=24,
    )(sums, block, stat_part, gram_part, row_moment[0], col_moment[0])

    pieces = update.reshape(owners, my_rows, order)
    returned = lax.all_to_all(pieces, "fsdp", split_axis=0, concat_axis=0, tiled=True)
    placed = call(
        place_kernel,
        shape((my_rows, owners * order), BF16),
        [SMEM, VMEM],
        VMEM,
        moved=4 * owners * my_rows * order,
    )(table, returned)
    return (placed[None], row_next[None], col_next[None])


def solution(mesh):
    in_specs = (
        P("grp", "fsdp", None),
        P("grp", None),
        P("grp", "fsdp", None, None),
        P("grp", "fsdp", None, None),
        P("grp", "fsdp", None, None),
        P("grp", "fsdp", None, None),
        P("grp", "fsdp", None),
        P("grp", "fsdp", None),
    )
    out_specs = (P("grp", "fsdp", None), P("grp", "fsdp", None), P("grp", "fsdp", None))
    return jax.shard_map(shards, mesh=mesh, in_specs=in_specs, out_specs=out_specs, check_vma=False)
```

```python
import functools

import jax
import jax.numpy as jnp
from jax import lax
from jax.experimental import pallas as pl
from jax.experimental.pallas import tpu as pltpu
from jax.sharding import PartitionSpec as P

DECAY_STAT = 0.95
DECAY_MOMENT = 0.95
CLIP_RMS = 0.5
EPSILON = 1e-08
F32 = jnp.float32
BF16 = jnp.bfloat16
TILE = 8
NB = 128
NT = NB // TILE
EXTRA = 16
CHUNKS = 4
NN = (((1,), (0,)), ((), ()))
NT_DIMS = (((1,), (1,)), ((), ()))
TN = (((0,), (0,)), ((), ()))


def mm(a, b, dims=NN):
    return lax.dot_general(a, b, dims, preferred_element_type=F32)


def mm_full(a, b, dims=NN):
    return lax.dot_general(a, b, dims, precision=lax.Precision.HIGHEST, preferred_element_type=F32)


def split3(x):
    high = x.astype(BF16)
    rest = x - high.astype(F32)
    mid = rest.astype(BF16)
    low = (rest - mid.astype(F32)).astype(BF16)
    return high, mid, low


def mm_split(x, exact, dims=NN):
    high, mid, low = split3(x)
    return mm(high, exact, dims) + mm(mid, exact, dims) + mm(low, exact, dims)


def lane(x, c):
    return jnp.broadcast_to(x[:, c : c + 1], (TILE, NB))


def row(x, r):
    return jnp.broadcast_to(x[r : r + 1, :], (TILE, NB))


def factor_steps(get, aug, side, out, slot):
    lanes = lax.broadcasted_iota(jnp.int32, (TILE, NB), 1)
    subs = lax.broadcasted_iota(jnp.int32, (TILE, NB), 0)

    def at(i):
        return (side, slice(TILE * i, TILE * i + TILE), slice(None))

    for i in range(NT):
        aug[at(i)] = jnp.where(lanes == subs + TILE * i, 1.0, 0.0).astype(F32)
    for k in range(NT):
        base = TILE * k
        tile = get[at(k)]
        both = aug[at(k)]
        forward = both
        cols = [lane(tile, base + j) for j in range(TILE)]
        pivots = jnp.ones((TILE, NB), F32)
        for j in range(TILE):
            pivot = row(cols[j], j)
            pivots = jnp.where(subs == j, pivot, pivots)
            mult = cols[j] * (1.0 / pivot)
            around = jnp.where(subs == j, 0.0, mult)
            below = jnp.where(subs > j, mult, 0.0)
            for q in range(j + 1, TILE):
                cols[q] = cols[q] - around * row(cols[q], j)
            both_row = row(both, j)
            tile = tile - around * row(tile, j)
            both = both - around * both_row
            forward = forward - below * both_row
            yield
        inverse = 1.0 / pivots
        out[slot + side, TILE * k : TILE * k + TILE, :] = forward * lax.rsqrt(pivots)
        tile = tile * inverse
        both = both * inverse
        tile_rows = [row(tile, j) for j in range(TILE)]
        both_rows = [row(both, j) for j in range(TILE)]
        for i in range(k + 1, NT):
            old = get[at(i)]
            left = [lane(old, base + j) for j in range(TILE)]
            first = [left[j] * tile_rows[j] for j in range(TILE)]
            second = [left[j] * both_rows[j] for j in range(TILE)]
            while len(first) > 1:
                first = [first[q] + first[q + 1] for q in range(0, len(first), 2)]
                second = [second[q] + second[q + 1] for q in range(0, len(second), 2)]
            get[at(i)] = old - first[0]
            aug[at(i)] = aug[at(i)] - second[0]
        yield


def interleave(steps, later, every):
    steps, later, count = list(steps), list(later), 0
    while steps or later:
        steps = [s for s in steps if next(s, steps) is not steps]
        count += 1
        if count % every == 0 or not steps:
            later = [s for s in later if next(s, later) is not later]


def prep_kernel(table_hbm, grad_hbm, out_ref, table_ref, grad_ref, table_sem, grad_sem):
    owners, _, width = out_ref.shape
    chunks, my_rows, span = grad_ref.shape
    order = chunks * span // owners
    table_copy = pltpu.make_async_copy(table_hbm, table_ref, table_sem)
    table_copy.start()
    copies = []
    for g in range(chunks):
        part = grad_hbm.at[:, g * span : (g + 1) * span]
        copies.append(pltpu.make_async_copy(part, grad_ref.at[g], grad_sem.at[g]))
        copies[g].start()
    table_copy.wait()
    total = jnp.zeros((my_rows, order), F32)
    for j in range(owners):
        g, first = divmod(j * order, span)
        if first == 0:
            copies[g].wait()
        part = grad_ref[g, :, first : first + order]
        for c in range(order // width):
            out_ref[table_ref[0, j], c * my_rows : (c + 1) * my_rows, :] = part[:, c * width : (c + 1) * width]
        wide = part.astype(F32)
        total = total + wide * wide
    high, mid, low = split3(jnp.broadcast_to(jnp.sum(total).reshape(1, 1), (EXTRA, width)))
    rows = lax.broadcasted_iota(jnp.int32, (EXTRA, width), 0)
    extra = jnp.where(rows == 0, high.astype(F32), jnp.where(rows == 1, mid.astype(F32), low.astype(F32)))
    extra = jnp.where(rows < 3, extra, 0.0).astype(BF16)
    for o in range(owners):
        out_ref[o, order // width * my_rows :, :] = extra


def sum_kernel(block_ref, sum_ref):
    owners, height, width = block_ref.shape
    total = jnp.zeros((EXTRA, width), F32)
    for o in range(owners):
        total = total + block_ref[o, height - EXTRA :, :].astype(F32)
    sum_ref[...] = jnp.broadcast_to(jnp.sum(total, axis=0).reshape(1, 1, width), sum_ref.shape)


def place_kernel(table_ref, back_ref, out_ref):
    owners, my_rows, order = back_ref.shape
    for j in range(owners):
        out_ref[:, j * order : (j + 1) * order] = back_ref[table_ref[0, j]]


def early_kernel(left_stat, right_stat, left_basis, right_basis, basis_t, stat_part):
    for side, (stat, basis) in enumerate(((left_stat, left_basis), (right_stat, right_basis))):
        turned = basis[...].T
        basis_t[side] = turned
        stat_part[side] = DECAY_STAT * mm(turned, stat[...])


def gram_kernel(recv_ref, basis_hbm, block_ref, gram_hbm, basis_t, gram_part, in_sem, out_sem):
    owners, height, width = recv_ref.shape
    order = block_ref.shape[0]
    my_rows = order // owners
    loads = [pltpu.make_async_copy(basis_hbm.at[s], basis_t.at[s], in_sem.at[s]) for s in range(2)]
    stores = [pltpu.make_async_copy(gram_part.at[s], gram_hbm.at[s], out_sem.at[s]) for s in range(2)]
    for load in loads:
        load.start()
    for o in range(owners):
        for c in range(order // width):
            piece = recv_ref[o, c * my_rows : (c + 1) * my_rows, :]
            block_ref[o * my_rows : (o + 1) * my_rows, c * width : (c + 1) * width] = piece
    block = block_ref[...]
    loads[0].wait()
    gram_part[0] = (1.0 - DECAY_STAT) * mm_split(mm(basis_t[0], block), block, NT_DIMS)
    stores[0].start()
    loads[1].wait()
    gram_part[1] = (1.0 - DECAY_STAT) * mm_split(mm(basis_t[1], block, NT_DIMS), block)
    stores[1].start()
    for store in stores:
        store.wait()


def main_kernel(
    count, sum_ref, block_ref, stat_part, gram_hbm, row_ref, col_ref, update_ref, row_out, col_out,
    gram_part, gram_sem, s_ref, a_ref, t_ref, aug_ref, w_ref, p_ref, q_ref,
):
    order = block_ref.shape[0]
    blocks = order // NB
    loads = [pltpu.make_async_copy(gram_hbm.at[s], gram_part.at[s], gram_sem.at[s]) for s in range(2)]
    for load in loads:
        load.start()
    total = jnp.sum(jnp.sum(sum_ref[...], axis=0), axis=1, keepdims=True) * (1.0 / sum_ref.shape[2])
    clip = CLIP_RMS / jnp.sqrt(total / count + 1e-06)
    for side in range(2):
        loads[side].wait()
        a = stat_part[side] + (clip * clip) * gram_part[side]
        a_ref[side] = a
        high, mid, low = split3(a)
        for k in range(blocks):
            part = slice(k * NB, order)
            mine = slice(k * NB, (k + 1) * NB)
            near = mm(low[mine], high[part], NT_DIMS) + mm(high[mine], low[part], NT_DIMS)
            near = near + mm(mid[mine], mid[part], NT_DIMS)
            near = near + mm(mid[mine], high[part], NT_DIMS) + mm(high[mine], mid[part], NT_DIMS)
            s_ref[side, mine, part] = near + mm(high[mine], high[part], NT_DIMS)

    def at(k):
        return slice(k * NB, (k + 1) * NB)

    def finish(k, side):
        w = w_ref[k % 2 * 2 + side]
        rest = slice((k + 1) * NB, order)
        if k + 2 < blocks:
            far = slice((k + 2) * NB, order)
            p_ref[side, :, far] = mm_full(w, s_ref[side, at(k), far])
            yield
        if k + 1 < blocks:
            panel_t = p_ref[side, :, rest].T
        half = order // 2
        for c in range(2):
            cols = slice(c * half, (c + 1) * half)
            turned = mm_full(w, a_ref[side, at(k), cols])
            q_ref[side, at(k), cols] = turned.astype(BF16)
            yield
            if k + 1 < blocks:
                a_ref[side, rest, cols] = a_ref[side, rest, cols] - mm_full(panel_t, turned)
                yield
        for i in range(k + 1, blocks):
            first = max(i, k + 2)
            if first < blocks:
                cols = slice(first * NB, order)
                panel_i = panel_t[(i - k - 1) * NB : (i - k) * NB]
                s_ref[side, at(i), cols] = s_ref[side, at(i), cols] - mm_full(panel_i, p_ref[side, :, cols])
                yield

    waiting = []
    for k in range(blocks):
        slot = k % 2 * 2
        for side in range(2):
            if k == 0:
                t_ref[side] = s_ref[side, at(0), at(0)]
        interleave([factor_steps(t_ref, aug_ref, side, w_ref, slot) for side in range(2)], waiting, 8)
        if k + 1 < blocks:
            for side in range(2):
                panel = mm_full(w_ref[slot + side], s_ref[side, at(k), at(k + 1)])
                p_ref[side, :, at(k + 1)] = panel
                t_ref[side] = s_ref[side, at(k + 1), at(k + 1)] - mm_full(panel.T, panel)
        waiting = [finish(k, side) for side in range(2)]
    interleave([], waiting, 1)

    block = block_ref[...]
    left_t = q_ref[0]
    right_t = q_ref[1]
    half = mm(left_t, block).astype(BF16)
    rotated = clip * mm(half, right_t, NT_DIMS)
    square = rotated * rotated
    col_next = DECAY_MOMENT * col_ref[...] + (1.0 - DECAY_MOMENT) * jnp.mean(square, axis=0, keepdims=True)
    old_rows = jnp.broadcast_to(row_ref[...], (NB, order)).T
    row_mean = jnp.broadcast_to(jnp.mean(square, axis=1, keepdims=True), (order, NB))
    row_next = DECAY_MOMENT * old_rows + (1.0 - DECAY_MOMENT) * row_mean
    col_out[...] = col_next
    across = row_next.T[0:1, :]
    row_out[...] = across
    second = row_next[:, 0:1] * col_next / jnp.mean(across)
    normed = (rotated / (jnp.sqrt(second) + EPSILON)).astype(BF16)
    back = mm(left_t, normed, TN).astype(BF16)
    update_ref[...] = mm(back, right_t).astype(BF16)


VMEM = pl.BlockSpec(memory_space=pltpu.VMEM)
SMEM = pl.BlockSpec(memory_space=pltpu.SMEM)
HBM = pl.BlockSpec(memory_space=pltpu.HBM)
DMA = pltpu.SemaphoreType.DMA


def call(kernel, out_shapes, in_specs, out_specs, scratch=(), flops=0, moved=0, limit=12):
    return pl.pallas_call(
        kernel,
        out_shape=out_shapes,
        in_specs=in_specs,
        out_specs=out_specs,
        scratch_shapes=list(scratch),
        compiler_params=pltpu.CompilerParams(vmem_limit_bytes=limit * 2**20),
        cost_estimate=pl.CostEstimate(flops=flops, bytes_accessed=moved, transcendentals=0),
    )


def shards(grad, table, left_stat, right_stat, left_basis, right_basis, row_moment, col_moment):
    order = left_stat.shape[-1]
    owners = lax.axis_size("fsdp")
    groups = lax.axis_size("grp")
    my_rows = grad.shape[1]
    shape = jax.ShapeDtypeStruct
    cube = 2 * order**3

    outgoing = call(
        prep_kernel,
        shape((owners, order // NB * my_rows + EXTRA, NB), BF16),
        [HBM, HBM],
        VMEM,
        [
            pltpu.SMEM(table.shape, jnp.int32),
            pltpu.VMEM((CHUNKS, my_rows, owners * order // CHUNKS), BF16),
            DMA,
            DMA((CHUNKS,)),
        ],
        moved=4 * owners * my_rows * order,
    )(table, grad[0])
    received = lax.all_to_all(outgoing, "fsdp", split_axis=0, concat_axis=0, tiled=True)

    basis_t, stat_part = call(
        early_kernel,
        (shape((2, order, order), BF16), shape((2, order, order), F32)),
        [VMEM] * 4,
        (VMEM, VMEM),
        flops=2 * cube,
        moved=16 * order * order,
    )(left_stat[0, 0], right_stat[0, 0], left_basis[0, 0], right_basis[0, 0])

    mine = call(sum_kernel, shape((groups, 1, NB), F32), [VMEM], VMEM, moved=64 * owners * NB)(received)
    sums = lax.all_to_all(mine, "grp", split_axis=0, concat_axis=0, tiled=True)

    wide = pltpu.VMEM((2, order, order), F32)
    block, gram_part = call(
        gram_kernel,
        (shape((order, order), BF16), shape((2, order, order), F32)),
        [VMEM, HBM],
        (VMEM, HBM),
        [pltpu.VMEM((2, order, order), BF16), wide, DMA((2,)), DMA((2,))],
        flops=8 * cube,
        moved=14 * order * order,
    )(received, basis_t)

    small = pltpu.VMEM((2, NB, NB), F32)
    update, row_next, col_next = call(
        functools.partial(main_kernel, float(groups * owners * order * order)),
        (shape((order, order), BF16), shape((1, order), F32), shape((1, order), F32)),
        [VMEM, VMEM, VMEM, HBM, VMEM, VMEM],
        (VMEM, VMEM, VMEM),
        [wide, DMA((2,)), wide, wide, small, small, pltpu.VMEM((4, NB, NB), F32), pltpu.VMEM((2, NB, order), F32), pltpu.VMEM((2, order, order), BF16)],
        flops=40 * cube,
        moved=20 * order * order,
        limit=24,
    )(sums, block, stat_part, gram_part, row_moment[0], col_moment[0])

    pieces = update.reshape(owners, my_rows, order)
    returned = lax.all_to_all(pieces, "fsdp", split_axis=0, concat_axis=0, tiled=True)
    placed = call(
        place_kernel,
        shape((my_rows, owners * order), BF16),
        [SMEM, VMEM],
        VMEM,
        moved=4 * owners * my_rows * order,
    )(table, returned)
    return (placed[None], row_next[None], col_next[None])


def solution(mesh):
    in_specs = (
        P("grp", "fsdp", None),
        P("grp", None),
        P("grp", "fsdp", None, None),
        P("grp", "fsdp", None, None),
        P("grp", "fsdp", None, None),
        P("grp", "fsdp", None, None),
        P("grp", "fsdp", None),
        P("grp", "fsdp", None),
    )
    out_specs = (P("grp", "fsdp", None), P("grp", "fsdp", None), P("grp", "fsdp", None))
    return jax.shard_map(shards, mesh=mesh, in_specs=in_specs, out_specs=out_specs, check_vma=False)
```

```python
import functools

import jax
import jax.numpy as jnp
from jax import lax
from jax.experimental import pallas as pl
from jax.experimental.pallas import tpu as pltpu
from jax.sharding import PartitionSpec as P

DECAY_STAT = 0.95
DECAY_MOMENT = 0.95
CLIP_RMS = 0.5
EPSILON = 1e-08
F32 = jnp.float32
BF16 = jnp.bfloat16
TILE = 8
NB = 128
NT = NB // TILE
EXTRA = 16
CHUNKS = 4
NN = (((1,), (0,)), ((), ()))
NT_DIMS = (((1,), (1,)), ((), ()))
TN = (((0,), (0,)), ((), ()))


def mm(a, b, dims=NN):
    return lax.dot_general(a, b, dims, preferred_element_type=F32)


def mm_full(a, b, dims=NN):
    return lax.dot_general(a, b, dims, precision=lax.Precision.HIGHEST, preferred_element_type=F32)


def split3(x):
    high = x.astype(BF16)
    rest = x - high.astype(F32)
    mid = rest.astype(BF16)
    low = (rest - mid.astype(F32)).astype(BF16)
    return high, mid, low


def mm_split(x, exact, dims=NN):
    high, mid, low = split3(x)
    return mm(high, exact, dims) + mm(mid, exact, dims) + mm(low, exact, dims)


def lane(x, c):
    return jnp.broadcast_to(x[:, c : c + 1], (TILE, NB))


def row(x, r):
    return jnp.broadcast_to(x[r : r + 1, :], (TILE, NB))


def factor_steps(get, aug, side, out, slot):
    lanes = lax.broadcasted_iota(jnp.int32, (TILE, NB), 1)
    subs = lax.broadcasted_iota(jnp.int32, (TILE, NB), 0)

    def at(i):
        return (side, slice(TILE * i, TILE * i + TILE), slice(None))

    for i in range(NT):
        aug[at(i)] = jnp.where(lanes == subs + TILE * i, 1.0, 0.0).astype(F32)
    for k in range(NT):
        base = TILE * k
        tile = get[at(k)]
        both = aug[at(k)]
        forward = both
        cols = [lane(tile, base + j) for j in range(TILE)]
        pivots = jnp.ones((TILE, NB), F32)
        for j in range(TILE):
            pivot = row(cols[j], j)
            pivots = jnp.where(subs == j, pivot, pivots)
            mult = cols[j] * (1.0 / pivot)
            around = jnp.where(subs == j, 0.0, mult)
            below = jnp.where(subs > j, mult, 0.0)
            for q in range(j + 1, TILE):
                cols[q] = cols[q] - around * row(cols[q], j)
            both_row = row(both, j)
            tile = tile - around * row(tile, j)
            both = both - around * both_row
            forward = forward - below * both_row
            yield
        inverse = 1.0 / pivots
        out[slot + side, TILE * k : TILE * k + TILE, :] = forward * lax.rsqrt(pivots)
        tile = tile * inverse
        both = both * inverse
        tile_rows = [row(tile, j) for j in range(TILE)]
        both_rows = [row(both, j) for j in range(TILE)]
        for i in range(k + 1, NT):
            old = get[at(i)]
            left = [lane(old, base + j) for j in range(TILE)]
            first = [left[j] * tile_rows[j] for j in range(TILE)]
            second = [left[j] * both_rows[j] for j in range(TILE)]
            while len(first) > 1:
                first = [first[q] + first[q + 1] for q in range(0, len(first), 2)]
                second = [second[q] + second[q + 1] for q in range(0, len(second), 2)]
            get[at(i)] = old - first[0]
            aug[at(i)] = aug[at(i)] - second[0]
        yield


def interleave(steps, later, every):
    steps, later, count = list(steps), list(later), 0
    while steps or later:
        steps = [s for s in steps if next(s, steps) is not steps]
        count += 1
        if count % every == 0 or not steps:
            later = [s for s in later if next(s, later) is not later]


def prep_kernel(table_hbm, grad_hbm, out_ref, table_ref, grad_ref, table_sem, grad_sem):
    owners, _, width = out_ref.shape
    chunks, my_rows, span = grad_ref.shape
    order = chunks * span // owners
    table_copy = pltpu.make_async_copy(table_hbm, table_ref, table_sem)
    table_copy.start()
    copies = []
    for g in range(chunks):
        part = grad_hbm.at[:, g * span : (g + 1) * span]
        copies.append(pltpu.make_async_copy(part, grad_ref.at[g], grad_sem.at[g]))
        copies[g].start()
    table_copy.wait()
    total = jnp.zeros((my_rows, order), F32)
    for j in range(owners):
        g, first = divmod(j * order, span)
        if first == 0:
            copies[g].wait()
        part = grad_ref[g, :, first : first + order]
        for c in range(order // width):
            out_ref[table_ref[0, j], c * my_rows : (c + 1) * my_rows, :] = part[:, c * width : (c + 1) * width]
        wide = part.astype(F32)
        total = total + wide * wide
    high, mid, low = split3(jnp.broadcast_to(jnp.sum(total).reshape(1, 1), (EXTRA, width)))
    rows = lax.broadcasted_iota(jnp.int32, (EXTRA, width), 0)
    extra = jnp.where(rows == 0, high.astype(F32), jnp.where(rows == 1, mid.astype(F32), low.astype(F32)))
    extra = jnp.where(rows < 3, extra, 0.0).astype(BF16)
    for o in range(owners):
        out_ref[o, order // width * my_rows :, :] = extra


def sum_kernel(block_ref, sum_ref):
    owners, height, width = block_ref.shape
    total = jnp.zeros((EXTRA, width), F32)
    for o in range(owners):
        total = total + block_ref[o, height - EXTRA :, :].astype(F32)
    sum_ref[...] = jnp.broadcast_to(jnp.sum(total, axis=0).reshape(1, 1, width), sum_ref.shape)


def place_kernel(table_ref, back_ref, out_ref):
    owners, my_rows, order = back_ref.shape
    for j in range(owners):
        out_ref[:, j * order : (j + 1) * order] = back_ref[table_ref[0, j]]


def early_kernel(left_stat, right_stat, left_basis, right_basis, basis_t, stat_part):
    for side, (stat, basis) in enumerate(((left_stat, left_basis), (right_stat, right_basis))):
        turned = basis[...].T
        basis_t[side] = turned
        stat_part[side] = DECAY_STAT * mm(turned, stat[...])


def gram_kernel(recv_ref, basis_t, block_ref, gram_part):
    owners, height, width = recv_ref.shape
    order = block_ref.shape[0]
    my_rows = order // owners
    for o in range(owners):
        for c in range(order // width):
            piece = recv_ref[o, c * my_rows : (c + 1) * my_rows, :]
            block_ref[o * my_rows : (o + 1) * my_rows, c * width : (c + 1) * width] = piece
    block = block_ref[...]
    gram_part[0] = (1.0 - DECAY_STAT) * mm_split(mm(basis_t[0], block), block, NT_DIMS)
    gram_part[1] = (1.0 - DECAY_STAT) * mm_split(mm(basis_t[1], block, NT_DIMS), block)


def main_kernel(
    count, sum_ref, block_ref, stat_part, gram_part, row_ref, col_ref, update_ref, row_out, col_out,
    s_ref, a_ref, t_ref, aug_ref, w_ref, p_ref, q_ref,
):
    order = block_ref.shape[0]
    blocks = order // NB
    total = jnp.sum(jnp.sum(sum_ref[...], axis=0), axis=1, keepdims=True) * (1.0 / sum_ref.shape[2])
    clip = CLIP_RMS / jnp.sqrt(total / count + 1e-06)
    for side in range(2):
        a = stat_part[side] + (clip * clip) * gram_part[side]
        a_ref[side] = a
        high, mid, low = split3(a)
        for k in range(blocks):
            part = slice(k * NB, order)
            mine = slice(k * NB, (k + 1) * NB)
            near = mm(low[mine], high[part], NT_DIMS) + mm(high[mine], low[part], NT_DIMS)
            near = near + mm(mid[mine], mid[part], NT_DIMS)
            near = near + mm(mid[mine], high[part], NT_DIMS) + mm(high[mine], mid[part], NT_DIMS)
            s_ref[side, mine, part] = near + mm(high[mine], high[part], NT_DIMS)

    def at(k):
        return slice(k * NB, (k + 1) * NB)

    def finish(k, side):
        w = w_ref[k % 2 * 2 + side]
        rest = slice((k + 1) * NB, order)
        if k + 2 < blocks:
            far = slice((k + 2) * NB, order)
            p_ref[side, :, far] = mm_full(w, s_ref[side, at(k), far])
            yield
        if k + 1 < blocks:
            panel_t = p_ref[side, :, rest].T
        half = order // 2
        for c in range(2):
            cols = slice(c * half, (c + 1) * half)
            turned = mm_full(w, a_ref[side, at(k), cols])
            q_ref[side, at(k), cols] = turned.astype(BF16)
            yield
            if k + 1 < blocks:
                a_ref[side, rest, cols] = a_ref[side, rest, cols] - mm_full(panel_t, turned)
                yield
        for i in range(k + 1, blocks):
            first = max(i, k + 2)
            if first < blocks:
                cols = slice(first * NB, order)
                panel_i = panel_t[(i - k - 1) * NB : (i - k) * NB]
                s_ref[side, at(i), cols] = s_ref[side, at(i), cols] - mm_full(panel_i, p_ref[side, :, cols])
                yield

    waiting = []
    for k in range(blocks):
        slot = k % 2 * 2
        for side in range(2):
            if k == 0:
                t_ref[side] = s_ref[side, at(0), at(0)]
        interleave([factor_steps(t_ref, aug_ref, side, w_ref, slot) for side in range(2)], waiting, 8)
        if k + 1 < blocks:
            for side in range(2):
                panel = mm_full(w_ref[slot + side], s_ref[side, at(k), at(k + 1)])
                p_ref[side, :, at(k + 1)] = panel
                t_ref[side] = s_ref[side, at(k + 1), at(k + 1)] - mm_full(panel.T, panel)
        waiting = [finish(k, side) for side in range(2)]
    interleave([], waiting, 1)

    block = block_ref[...]
    left_t = q_ref[0]
    right_t = q_ref[1]
    half = mm(left_t, block).astype(BF16)
    rotated = clip * mm(half, right_t, NT_DIMS)
    square = rotated * rotated
    col_next = DECAY_MOMENT * col_ref[...] + (1.0 - DECAY_MOMENT) * jnp.mean(square, axis=0, keepdims=True)
    old_rows = jnp.broadcast_to(row_ref[...], (NB, order)).T
    row_mean = jnp.broadcast_to(jnp.mean(square, axis=1, keepdims=True), (order, NB))
    row_next = DECAY_MOMENT * old_rows + (1.0 - DECAY_MOMENT) * row_mean
    col_out[...] = col_next
    across = row_next.T[0:1, :]
    row_out[...] = across
    second = row_next[:, 0:1] * col_next / jnp.mean(across)
    normed = (rotated / (jnp.sqrt(second) + EPSILON)).astype(BF16)
    back = mm(left_t, normed, TN).astype(BF16)
    update_ref[...] = mm(back, right_t).astype(BF16)


VMEM = pl.BlockSpec(memory_space=pltpu.VMEM)
SMEM = pl.BlockSpec(memory_space=pltpu.SMEM)
HBM = pl.BlockSpec(memory_space=pltpu.HBM)
DMA = pltpu.SemaphoreType.DMA


def call(kernel, out_shapes, in_specs, out_specs, scratch=(), flops=0, moved=0, limit=12):
    return pl.pallas_call(
        kernel,
        out_shape=out_shapes,
        in_specs=in_specs,
        out_specs=out_specs,
        scratch_shapes=list(scratch),
        compiler_params=pltpu.CompilerParams(vmem_limit_bytes=limit * 2**20),
        cost_estimate=pl.CostEstimate(flops=flops, bytes_accessed=moved, transcendentals=0),
    )


def shards(grad, table, left_stat, right_stat, left_basis, right_basis, row_moment, col_moment):
    order = left_stat.shape[-1]
    owners = lax.axis_size("fsdp")
    groups = lax.axis_size("grp")
    my_rows = grad.shape[1]
    shape = jax.ShapeDtypeStruct
    cube = 2 * order**3

    outgoing = call(
        prep_kernel,
        shape((owners, order // NB * my_rows + EXTRA, NB), BF16),
        [HBM, HBM],
        VMEM,
        [
            pltpu.SMEM(table.shape, jnp.int32),
            pltpu.VMEM((CHUNKS, my_rows, owners * order // CHUNKS), BF16),
            DMA,
            DMA((CHUNKS,)),
        ],
        moved=4 * owners * my_rows * order,
        limit=63,
    )(table, grad[0])
    received = lax.all_to_all(outgoing, "fsdp", split_axis=0, concat_axis=0, tiled=True)

    basis_t, stat_part = call(
        early_kernel,
        (shape((2, order, order), BF16), shape((2, order, order), F32)),
        [VMEM] * 4,
        (VMEM, VMEM),
        flops=2 * cube,
        moved=16 * order * order,
    )(left_stat[0, 0], right_stat[0, 0], left_basis[0, 0], right_basis[0, 0])

    mine = call(sum_kernel, shape((groups, 1, NB), F32), [VMEM], VMEM, moved=64 * owners * NB)(received)
    sums = lax.all_to_all(mine, "grp", split_axis=0, concat_axis=0, tiled=True)

    block, gram_part = call(
        gram_kernel,
        (shape((order, order), BF16), shape((2, order, order), F32)),
        [VMEM, VMEM],
        (VMEM, VMEM),
        flops=8 * cube,
        moved=14 * order * order,
    )(received, basis_t)

    wide = pltpu.VMEM((2, order, order), F32)
    small = pltpu.VMEM((2, NB, NB), F32)
    update, row_next, col_next = call(
        functools.partial(main_kernel, float(groups * owners * order * order)),
        (shape((order, order), BF16), shape((1, order), F32), shape((1, order), F32)),
        [VMEM] * 6,
        (VMEM, VMEM, VMEM),
        [wide, wide, small, small, pltpu.VMEM((4, NB, NB), F32), pltpu.VMEM((2, NB, order), F32), pltpu.VMEM((2, order, order), BF16)],
        flops=40 * cube,
        moved=20 * order * order,
        limit=24,
    )(sums, block, stat_part, gram_part, row_moment[0], col_moment[0])

    pieces = update.reshape(owners, my_rows, order)
    returned = lax.all_to_all(pieces, "fsdp", split_axis=0, concat_axis=0, tiled=True)
    placed = call(
        place_kernel,
        shape((my_rows, owners * order), BF16),
        [SMEM, VMEM],
        VMEM,
        moved=4 * owners * my_rows * order,
    )(table, returned)
    return (placed[None], row_next[None], col_next[None])


def solution(mesh):
    in_specs = (
        P("grp", "fsdp", None),
        P("grp", None),
        P("grp", "fsdp", None, None),
        P("grp", "fsdp", None, None),
        P("grp", "fsdp", None, None),
        P("grp", "fsdp", None, None),
        P("grp", "fsdp", None),
        P("grp", "fsdp", None),
    )
    out_specs = (P("grp", "fsdp", None), P("grp", "fsdp", None), P("grp", "fsdp", None))
    return jax.shard_map(shards, mesh=mesh, in_specs=in_specs, out_specs=out_specs, check_vma=False)
```
